32 devices in a mesh: dp: 4 (over y, x), rows: 8 (over z, core).
Axes of the slice: x: 2, y: 2, z: 4, core: 2. Of those that a mesh axis runs over, the one named last changes fastest.
Arguments:
- images: float32 [8192, 1152], P(('dp', 'rows')), may hold values from -0.2 to 0.2
- texts: float32 [8192, 1152], P(('dp', 'rows')), may hold values from -0.2 to 0.2
- log_temp: float32 [1], replicated, may hold values from 0.7 to 1.8
- bias: float32 [1], replicated, may hold values from -3 to -1
Outputs:
- row_loss: float32 [8192], P(('dp', 'rows'))
- image_grad: float32 [8192, 1152], P(('dp', 'rows'))
- text_grad: float32 [8192, 1152], P(('dp', 'rows'))
The draws below stay inside these ranges and needn't reach their ends.
All inputs are finite; a program needn't handle non-finite values.
Results may differ from the reference program's by a relative error of at most 0.0091.
Values may be sent and summed in bfloat16 or wider, within the bound.
A program may use at most 64 MiB of HBM per device.

```python
import jax
import jax.numpy as jnp
from jax import lax

D = 1152
ROWS_DEV = 256
STEPS = 4
BLOCKS = 32
PAIRS = 8192


def level_of(stream_key, shape, split, smallest, largest):
    loudness = 1.0
    for position, shards_of in split:
        draws = jax.random.uniform(jax.random.fold_in(jax.random.fold_in(stream_key, 6), position), (shards_of,), jnp.float32, smallest / len(split), largest / len(split))
        loudness = loudness * jnp.repeat(jnp.exp(draws), shape[position] // shards_of).reshape((-1,) + (1,) * (len(shape) - 1 - position))
    return loudness


def bell_draw(stream_key, extent, deviation, bound, split=(), kind=jnp.bfloat16):
    drawn = jax.random.normal(stream_key, extent, jnp.float32) * deviation
    if len(split) > 0:
        drawn = level_of(stream_key, extent, split, -0.22, 0.18) * drawn
    return jnp.clip(drawn, min=-bound, max=bound).astype(kind)


def setup_inputs(seed: int = 0) -> dict:
    streams_of = jax.random.split(jax.random.key(seed), 5)
    images = bell_draw(streams_of[0], (PAIRS, D), (1.0 / 32), 0.2, ((0, 32),), jnp.float32)
    texts = bell_draw(streams_of[1], (PAIRS, D), (1.0 / 32), 0.2, ((0, 32),), jnp.float32)
    log_temp = jnp.clip(jax.random.uniform(streams_of[2], (1,), jnp.float32, 0.7, 1.8), 0.7, 1.8)
    bias = jnp.clip(jax.random.uniform(streams_of[3], (1,), jnp.float32, -3.0, -1.0), -3.0, -1.0)
    return dict(images=images, texts=texts, log_temp=log_temp, bias=bias)


def unit_rows(values):
    norms = jnp.sqrt(lax.optimization_barrier(jnp.sum(values * values, axis=-1, keepdims=True)) + 1e-06)
    return (values / norms, norms)

def back_rows(unit, norms, grad_unit):
    along = lax.optimization_barrier(jnp.sum(unit * grad_unit, axis=-1, keepdims=True))
    return (grad_unit - unit * along) / norms

def reference(images, texts, log_temp, bias):
    scale = jnp.exp(log_temp[0])
    shift_b = bias[0]
    img_unit, img_norm = unit_rows(images)
    txt_unit, txt_norm = unit_rows(texts)
    img_half = img_unit.astype(jnp.bfloat16).reshape(BLOCKS, ROWS_DEV, D)
    txt_half = txt_unit.astype(jnp.bfloat16).reshape(BLOCKS, ROWS_DEV, D)
    img_wide = img_half.astype(jnp.float32)
    eye = jnp.eye(ROWS_DEV, dtype=jnp.float32)
    loss_sum = jnp.zeros((BLOCKS, ROWS_DEV), jnp.float32)
    img_grad_unit = jnp.zeros((BLOCKS, ROWS_DEV, D), jnp.float32)
    txt_grad_unit = jnp.zeros((BLOCKS, ROWS_DEV, D), jnp.float32)
    for step in range(STEPS):
        visit = jnp.roll(txt_half, step, axis=0).astype(jnp.float32)
        logits = scale * jnp.einsum('bik,bjk->bij', img_wide, visit) + shift_b
        if step == 0:
            sign = 2.0 * eye - 1.0
        else:
            sign = -jnp.ones_like(eye)
        loss_sum = loss_sum + lax.optimization_barrier(jnp.sum(jax.nn.softplus(-sign * logits), axis=-1))
        dlogit = (-sign * jax.nn.sigmoid(-sign * logits) * scale).astype(jnp.bfloat16).astype(jnp.float32)
        img_grad_unit = img_grad_unit + jnp.einsum('bij,bjk->bik', dlogit, visit)
        part = jnp.einsum('bij,bik->bjk', dlogit, img_wide)
        txt_grad_unit = txt_grad_unit + jnp.roll(part, -step, axis=0)
    row_loss = (loss_sum / (STEPS * ROWS_DEV)).reshape(PAIRS)
    image_grad = back_rows(img_unit, img_norm, img_grad_unit.reshape(PAIRS, D))
    text_grad = back_rows(txt_unit, txt_norm, txt_grad_unit.reshape(PAIRS, D))
    return (row_loss, image_grad, text_grad)
```

```python
import functools

import jax
import jax.numpy as jnp
from jax import lax
from jax.experimental import pallas as pl
from jax.experimental.pallas import tpu as pltpu
from jax.sharding import PartitionSpec as P

STEPS = 4
CHUNKS = 8
MESH = pl.DeviceIdType.MESH


def kernel(img_hbm, txt_hbm, temp_ref, bias_ref, loss_ref, gimg_ref, gtxt_ref,
           xin, own, buf, acc, losses, inv, in_sem, send_sem, recv_sem, out_sem):
    rows_n = lax.axis_size("rows")
    total = lax.axis_size("dp") * rows_n
    me = lax.axis_index("dp") * rows_n + lax.axis_index("rows")
    p = lax.rem(me, 2)
    q = 1 - p
    d = 1 - 2 * p
    count = own.shape[1]
    part = count // CHUNKS

    def peer(offset):
        place = lax.rem(me + offset * d + total, total)
        return (lax.div(place, rows_n), lax.rem(place, rows_n))

    barrier = pltpu.get_barrier_semaphore()
    for offset in (1, 2, 3, -1, -2):
        pl.semaphore_signal(barrier, inc=1, device_id=peer(offset), device_id_type=MESH)

    loads = [pltpu.make_async_copy(txt_hbm, xin.at[0], in_sem.at[0]),
             pltpu.make_async_copy(img_hbm, xin.at[1], in_sem.at[1])]
    for load in loads:
        load.start()

    def normalise(kind):
        values = xin[kind]
        scale_back = 1.0 / jnp.sqrt(jnp.sum(values * values, axis=-1, keepdims=True) + 1e-06)
        inv[kind] = jnp.broadcast_to(scale_back, inv.shape[1:])
        own[kind] = (values * scale_back).astype(jnp.bfloat16)

    def rows_of(i):
        return pl.ds(i * part, part)

    def remote(src, kind, slot, rows, number, i, offset):
        return pltpu.make_async_remote_copy(
            src_ref=src.at[rows], dst_ref=buf.at[kind, slot, rows],
            send_sem=send_sem.at[number, i], recv_sem=recv_sem.at[kind, slot, i],
            device_id=peer(offset), device_id_type=MESH)

    def landed(kind, slot, rows, i):
        pltpu.make_async_remote_copy(
            src_ref=buf.at[kind, slot, rows], dst_ref=buf.at[kind, slot, rows],
            send_sem=send_sem.at[0, i], recv_sem=recv_sem.at[kind, slot, i],
            device_id=peer(1), device_id_type=MESH).wait_recv()

    everything = pl.ds(0, count)
    scale = jnp.exp(temp_ref[...])
    shift = bias_ref[...]

    def tile(kind, visit, first):
        other = visit[...]
        dots = lax.dot_general(own[1 - kind], other, (((1,), (1,)), ((), ())),
                               preferred_element_type=jnp.float32)
        z = scale * dots + shift
        if first:
            eye = (lax.broadcasted_iota(jnp.int32, z.shape, 0)
                   == lax.broadcasted_iota(jnp.int32, z.shape, 1))
            z = jnp.where(eye, -z, z)
        e = jnp.exp(z)
        more = 1.0 + e
        soft = jnp.log(more)
        slope = (e / more) * scale
        if first:
            slope = jnp.where(eye, -slope, slope)
        half = soft.shape[1] // 2
        folded = soft[:, :half] + soft[:, half:]
        grad = jnp.dot(slope.astype(jnp.bfloat16), other, preferred_element_type=jnp.float32)
        if first:
            losses[kind] = folded
            acc[kind] = grad
        else:
            losses[kind] = losses[kind] + folded
            acc[kind] = acc[kind] + grad

    sent = []

    def send(copy):
        copy.start()
        sent.append(copy)

    pltpu.make_async_copy(txt_hbm, xin.at[q], in_sem.at[q]).wait()
    normalise(q)
    pl.semaphore_wait(barrier, 5)
    for i in range(CHUNKS):
        send(remote(own.at[q], q, 0, rows_of(i), 0, i, -1))
    pltpu.make_async_copy(txt_hbm, xin.at[p], in_sem.at[p]).wait()
    normalise(p)
    send(remote(own.at[p], p, 0, everything, 1, 0, 1))

    tile(0, own.at[0], True)
    tile(1, own.at[1], True)
    landed(q, 0, everything, 0)
    tile(q, buf.at[q, 0], False)

    for i in range(CHUNKS):
        rows = rows_of(i)
        landed(p, 0, rows, i)
        send(remote(buf.at[p, 0], p, 2, rows, 2, i, 2))
        send(remote(buf.at[p, 0], p, 1, rows, 3, i, 1))
        send(remote(own.at[p], p, 2, rows, 4, i, 3))
        if i > 0:
            landed(q, 2, rows_of(i - 1), i - 1)
            send(remote(buf.at[q, 2], q, 1, rows_of(i - 1), 5, i - 1, 1))
    tile(p, buf.at[p, 0], False)
    landed(q, 2, rows_of(CHUNKS - 1), CHUNKS - 1)
    send(remote(buf.at[q, 2], q, 1, rows_of(CHUNKS - 1), 5, CHUNKS - 1, 1))
    for kind, slot in ((q, 1), (q, 2), (p, 1), (p, 2)):
        if (kind is q and slot == 2) is False:
            for i in range(CHUNKS):
                landed(kind, slot, rows_of(i), i)
        tile(kind, buf.at[kind, slot], False)

    loss_ref[...] = jnp.sum(losses[0].T, axis=0, keepdims=True) / (STEPS * count)
    for kind, out in ((0, gimg_ref), (1, gtxt_ref)):
        factor = inv[1 - kind][:, :1]
        unit = xin[1 - kind] * factor
        grad = acc[kind]
        along = jnp.sum(unit * grad, axis=-1, keepdims=True)
        out[...] = (grad - unit * along) * factor
    for copy in sent:
        copy.wait_send()


def local(images, texts, log_temp, bias):
    count, width = images.shape
    block = jax.ShapeDtypeStruct((count, width), jnp.float32)
    vmem = pl.BlockSpec(memory_space=pltpu.VMEM)
    hbm = pl.BlockSpec(memory_space=pl.ANY)
    loss, gimg, gtxt = pl.pallas_call(
        kernel,
        out_shape=(jax.ShapeDtypeStruct((1, count), jnp.float32), block, block),
        in_specs=[hbm, hbm, vmem, vmem],
        out_specs=(vmem, vmem, vmem),
        scratch_shapes=[
            pltpu.VMEM((2, count, width), jnp.float32),
            pltpu.VMEM((2, count, width), jnp.bfloat16),
            pltpu.VMEM((2, STEPS - 1, count, width), jnp.bfloat16),
            pltpu.VMEM((2, count, width), jnp.float32),
            pltpu.VMEM((2, count, count // 2), jnp.float32),
            pltpu.VMEM((2, count, 128), jnp.float32),
            pltpu.SemaphoreType.DMA((2,)),
            pltpu.SemaphoreType.DMA((6, CHUNKS)),
            pltpu.SemaphoreType.DMA((2, STEPS - 1, CHUNKS)),
            pltpu.SemaphoreType.DMA((2,)),
        ],
        compiler_params=pltpu.CompilerParams(
            collective_id=0, has_side_effects=True, vmem_limit_bytes=48 * 1024 * 1024),
    )(images, texts, log_temp.reshape(1, 1), bias.reshape(1, 1))
    return (loss.reshape(count), gimg, gtxt)


def solution(mesh):
    placed = (P(("dp", "rows"), None), P(("dp", "rows"), None), P(), P())
    return jax.shard_map(
        local,
        mesh=mesh,
        in_specs=placed,
        out_specs=(P(("dp", "rows")), P(("dp", "rows"), None), P(("dp", "rows"), None)),
        check_vma=False,
    )
```

```python
import functools

import jax
import jax.numpy as jnp
from jax import lax
from jax.experimental import pallas as pl
from jax.experimental.pallas import tpu as pltpu
from jax.sharding import PartitionSpec as P

STEPS = 4
CHUNKS = 8
HALVES = 2
LOADS = 4
PEERS = (1, 2, 3, -1, -2, -3)
MESH = pl.DeviceIdType.MESH


def kernel(img_hbm, txt_hbm, temp_ref, bias_ref, loss_ref, gimg_ref, gtxt_ref,
           xin, own, buf, acc, losses, inv, in_sem, send_sem, recv_sem):
    rows_n = lax.axis_size("rows")
    total = lax.axis_size("dp") * rows_n
    me = lax.axis_index("dp") * rows_n + lax.axis_index("rows")
    p = lax.rem(me, 2)
    q = 1 - p
    d = 1 - 2 * p
    count = own.shape[1]
    part = count // CHUNKS

    def peer(offset):
        place = lax.rem(me + offset * d + total, total)
        return (lax.div(place, rows_n), lax.rem(place, rows_n))

    barrier = pltpu.get_barrier_semaphore()
    for offset in PEERS:
        pl.semaphore_signal(barrier, inc=1, device_id=peer(offset), device_id_type=MESH)

    piece = count // LOADS

    def loading(source, kind, j):
        rows = pl.ds(j * piece, piece)
        return pltpu.make_async_copy(source.at[rows], xin.at[kind, rows], in_sem.at[kind, j])

    for j in range(LOADS):
        loading(txt_hbm, 0, j).start()
        loading(img_hbm, 1, j).start()

    def normalise(kind, j):
        rows = pl.ds(j * piece, piece)
        loading(txt_hbm, kind, j).wait()
        values = xin[kind, rows]
        scale_back = 1.0 / jnp.sqrt(jnp.sum(values * values, axis=-1, keepdims=True) + 1e-06)
        inv[kind, rows] = jnp.broadcast_to(scale_back, (piece, inv.shape[2]))
        own[kind, rows] = (values * scale_back).astype(jnp.bfloat16)

    line = rows_n // 2
    spot = lax.rem(lax.div(me, 2), line)

    def crosses(at, way):
        return jnp.logical_or(at + way < 0, at + way >= line)

    leaving = crosses(spot, d)
    early = jnp.logical_or(leaving, crosses(spot, -d))
    direct = crosses(lax.rem(spot - d + line, line), -d)

    def rows_of(i):
        return pl.ds(i * part, part)

    def remote(src, kind, slot, rows, number, i, offset):
        return pltpu.make_async_remote_copy(
            src_ref=src.at[rows], dst_ref=buf.at[kind, slot, rows],
            send_sem=send_sem.at[number, i], recv_sem=recv_sem.at[kind, slot, i],
            device_id=peer(offset), device_id_type=MESH)

    def landed(kind, slot, rows, i):
        pltpu.make_async_remote_copy(
            src_ref=buf.at[kind, slot, rows], dst_ref=buf.at[kind, slot, rows],
            send_sem=send_sem.at[0, i], recv_sem=recv_sem.at[kind, slot, i],
            device_id=peer(1), device_id_type=MESH).wait_recv()

    everything = pl.ds(0, count)
    scale = jnp.exp(jnp.full((1, 1), temp_ref[0], jnp.float32))
    shift = bias_ref[0]

    def tile(kind, visit, first):
        other = visit[...]
        dots = lax.dot_general(own[1 - kind], other, (((1,), (1,)), ((), ())),
                               preferred_element_type=jnp.float32)
        z = scale * dots + shift
        if first:
            eye = (lax.broadcasted_iota(jnp.int32, z.shape, 0)
                   == lax.broadcasted_iota(jnp.int32, z.shape, 1))
            z = jnp.where(eye, -z, z)
        e = jnp.exp(z)
        more = 1.0 + e
        soft = jnp.log(more)
        slope = (e / more) * scale
        if first:
            slope = jnp.where(eye, -slope, slope)
        wide = losses.shape[2]
        folded = soft[:, :wide]
        if first:
            for at in range(wide, count, wide):
                folded = folded + soft[:, at:at + wide]
        grad = jnp.dot(slope.astype(jnp.bfloat16), other, preferred_element_type=jnp.float32)
        if first:
            losses[kind] = folded
            acc[kind] = grad
        else:
            losses[kind] = losses[kind] + folded
            acc[kind] = acc[kind] + grad

    sent = []

    def send(copy, when=None):
        if when is None:
            copy.start()
        else:
            pl.when(when)(copy.start)
        sent.append((copy, when))

    for j in range(LOADS):
        normalise(q, j)
    pl.semaphore_wait(barrier, len(PEERS))
    for i in range(CHUNKS):
        send(remote(own.at[q], q, 2, rows_of(i), 6, i, -3), direct)
        send(remote(own.at[q], q, 0, rows_of(i), 0, i, -1))
    for j in range(LOADS):
        normalise(p, j)
    for i in range(CHUNKS):
        send(remote(own.at[p], p, 2, rows_of(i), 4, i, 3), early)
    send(remote(own.at[p], p, 0, everything, 1, 0, 1))

    tile(0, own.at[0], True)
    tile(1, own.at[1], True)
    span = count // HALVES

    def half_tile(kind, slot, h):
        tile(kind, buf.at[kind, slot, pl.ds(h * span, span)], False)

    landed(q, 0, everything, 0)
    for h in range(HALVES):
        half_tile(q, 0, h)

    late = jnp.logical_not(early)
    staying = jnp.logical_not(leaving)
    per = CHUNKS // HALVES

    def pass_on(i):
        landed(q, 2, rows_of(i), i)
        send(remote(buf.at[q, 2], q, 1, rows_of(i), 5, i, 1))

    for i in range(CHUNKS):
        rows = rows_of(i)
        landed(p, 0, rows, i)
        send(remote(buf.at[p, 0], p, 2, rows, 2, i, 2), staying)
        send(remote(buf.at[p, 0], p, 1, rows, 3, i, 1))
        again = remote(own.at[p], p, 2, rows, 4, i, 3)
        pl.when(late)(again.start)
        if i > 0:
            pass_on(i - 1)
        if i % per == per - 1:
            half_tile(p, 0, i // per)
        if i > 0 and (i - 1) % per == per - 1:
            half_tile(q, 2, (i - 1) // per)
    pass_on(CHUNKS - 1)
    half_tile(q, 2, HALVES - 1)
    for kind, slot in ((q, 1), (p, 1), (p, 2)):
        for h in range(HALVES):
            for i in range(h * per, (h + 1) * per):
                landed(kind, slot, rows_of(i), i)
            half_tile(kind, slot, h)

    loss_ref[...] = jnp.sum(losses[0].T, axis=0, keepdims=True) / (STEPS * count)
    for kind, out in ((0, gimg_ref), (1, gtxt_ref)):
        factor = inv[1 - kind][:, :1]
        unit = xin[1 - kind] * factor
        grad = acc[kind]
        along = jnp.sum(unit * grad, axis=-1, keepdims=True)
        out[...] = (grad - unit * along) * factor
    for copy, when in sent:
        if when is None or when is early:
            copy.wait_send()
        else:
            pl.when(when)(copy.wait_send)


def local(images, texts, log_temp, bias):
    count, width = images.shape
    block = jax.ShapeDtypeStruct((count, width), jnp.float32)
    vmem = pl.BlockSpec(memory_space=pltpu.VMEM)
    smem = pl.BlockSpec(memory_space=pltpu.SMEM)
    hbm = pl.BlockSpec(memory_space=pl.ANY)
    loss, gimg, gtxt = pl.pallas_call(
        kernel,
        out_shape=(jax.ShapeDtypeStruct((1, count), jnp.float32), block, block),
        in_specs=[hbm, hbm, smem, smem],
        out_specs=(vmem, vmem, vmem),
        scratch_shapes=[
            pltpu.VMEM((2, count, width), jnp.float32),
            pltpu.VMEM((2, count, width), jnp.bfloat16),
            pltpu.VMEM((2, STEPS - 1, count, width), jnp.bfloat16),
            pltpu.VMEM((2, count, width), jnp.float32),
            pltpu.VMEM((2, count, count // HALVES), jnp.float32),
            pltpu.VMEM((2, count, 128), jnp.float32),
            pltpu.SemaphoreType.DMA((2, LOADS)),
            pltpu.SemaphoreType.DMA((7, CHUNKS)),
            pltpu.SemaphoreType.DMA((2, STEPS - 1, CHUNKS)),
        ],
        compiler_params=pltpu.CompilerParams(
            collective_id=0, has_side_effects=True, vmem_limit_bytes=62 * 1024 * 1024),
    )(images, texts, log_temp, bias)
    return (loss.reshape(count), gimg, gtxt)


def solution(mesh):
    placed = (P(("dp", "rows"), None), P(("dp", "rows"), None), P(), P())
    return jax.shard_map(
        local,
        mesh=mesh,
        in_specs=placed,
        out_specs=(P(("dp", "rows")), P(("dp", "rows"), None), P(("dp", "rows"), None)),
        check_vma=False,
    )
```

```python
import functools

import jax
import jax.numpy as jnp
from jax import lax
from jax.experimental import pallas as pl
from jax.experimental.pallas import tpu as pltpu
from jax.sharding import PartitionSpec as P

STEPS = 4
CHUNKS = 8
HALVES = 2
LOADS = 4
LAG = 6
PEERS = (1, 2, 3, -1, -2, -3)
MESH = pl.DeviceIdType.MESH


def kernel(img_hbm, txt_hbm, temp_ref, bias_ref, loss_ref, gimg_ref, gtxt_ref,
           xin, own, buf, acc, losses, inv, in_sem, send_sem, recv_sem):
    rows_n = lax.axis_size("rows")
    total = lax.axis_size("dp") * rows_n
    me = lax.axis_index("dp") * rows_n + lax.axis_index("rows")
    p = lax.rem(me, 2)
    q = 1 - p
    d = 1 - 2 * p
    count = own.shape[1]
    part = count // CHUNKS

    def peer(offset):
        place = lax.rem(me + offset * d + total, total)
        return (lax.div(place, rows_n), lax.rem(place, rows_n))

    barrier = pltpu.get_barrier_semaphore()
    for offset in PEERS:
        pl.semaphore_signal(barrier, inc=1, device_id=peer(offset), device_id_type=MESH)

    piece = count // LOADS

    def loading(source, kind, j):
        rows = pl.ds(j * piece, piece)
        return pltpu.make_async_copy(source.at[rows], xin.at[kind, rows], in_sem.at[kind, j])

    for j in range(LOADS):
        loading(txt_hbm, 0, j).start()
        loading(img_hbm, 1, j).start()

    def normalise(kind, j):
        rows = pl.ds(j * piece, piece)
        loading(txt_hbm, kind, j).wait()
        values = xin[kind, rows]
        scale_back = 1.0 / jnp.sqrt(jnp.sum(values * values, axis=-1, keepdims=True) + 1e-06)
        inv[kind, rows] = jnp.broadcast_to(scale_back, (piece, inv.shape[2]))
        own[kind, rows] = (values * scale_back).astype(jnp.bfloat16)

    line = rows_n // 2
    spot = lax.rem(lax.div(me, 2), line)

    def crosses(at, way):
        return jnp.logical_or(at + way < 0, at + way >= line)

    leaving = crosses(spot, d)
    direct = crosses(lax.rem(spot - d + line, line), -d)

    def rows_of(i):
        return pl.ds(i * part, part)

    def remote(src, kind, slot, rows, number, i, offset):
        return pltpu.make_async_remote_copy(
            src_ref=src.at[rows], dst_ref=buf.at[kind, slot, rows],
            send_sem=send_sem.at[number, i], recv_sem=recv_sem.at[kind, slot, i],
            device_id=peer(offset), device_id_type=MESH)

    def landed(kind, slot, rows, i):
        pltpu.make_async_remote_copy(
            src_ref=buf.at[kind, slot, rows], dst_ref=buf.at[kind, slot, rows],
            send_sem=send_sem.at[0, i], recv_sem=recv_sem.at[kind, slot, i],
            device_id=peer(1), device_id_type=MESH).wait_recv()

    everything = pl.ds(0, count)
    scale = jnp.exp(jnp.full((1, 1), temp_ref[0], jnp.float32))
    shift = bias_ref[0]

    def tile(kind, visit, first):
        other = visit[...]
        dots = lax.dot_general(own[1 - kind], other, (((1,), (1,)), ((), ())),
                               preferred_element_type=jnp.float32)
        z = scale * dots + shift
        if first:
            eye = (lax.broadcasted_iota(jnp.int32, z.shape, 0)
                   == lax.broadcasted_iota(jnp.int32, z.shape, 1))
            z = jnp.where(eye, -z, z)
        e = jnp.exp(z)
        more = 1.0 + e
        soft = jnp.log(more)
        slope = (e / more) * scale
        if first:
            slope = jnp.where(eye, -slope, slope)
        wide = losses.shape[2]
        folded = soft[:, :wide]
        if first:
            for at in range(wide, count, wide):
                folded = folded + soft[:, at:at + wide]
        grad = jnp.dot(slope.astype(jnp.bfloat16), other, preferred_element_type=jnp.float32)
        if first:
            losses[kind] = folded
            acc[kind] = grad
        else:
            losses[kind] = losses[kind] + folded
            acc[kind] = acc[kind] + grad

    sent = []

    def send(copy, when=None):
        if when is None:
            copy.start()
        else:
            pl.when(when)(copy.start)
        sent.append((copy, when))

    for j in range(LOADS):
        normalise(q, j)
    pl.semaphore_wait(barrier, len(PEERS))
    for i in range(CHUNKS):
        send(remote(own.at[q], q, 0, rows_of(i), 0, i, -1))
    for j in range(LOADS):
        normalise(p, j)
    send(remote(own.at[p], p, 0, everything, 1, 0, 1))

    tile(0, own.at[0], True)
    tile(1, own.at[1], True)
    span = count // HALVES

    def half_tile(kind, slot, h):
        tile(kind, buf.at[kind, slot, pl.ds(h * span, span)], False)

    landed(q, 0, everything, 0)
    for h in range(HALVES):
        half_tile(q, 0, h)

    staying = jnp.logical_not(leaving)
    per = CHUNKS // HALVES

    def second_wave(i):
        rows = rows_of(i)
        send(remote(buf.at[p, 0], p, 2, rows, 2, i, 2), staying)
        send(remote(own.at[p], p, 2, rows, 4, i, 3))
        send(remote(own.at[q], q, 2, rows, 6, i, -3), direct)

    def pass_on(i):
        landed(q, 2, rows_of(i), i)
        send(remote(buf.at[q, 2], q, 1, rows_of(i), 5, i, 1))

    for i in range(CHUNKS):
        landed(p, 0, rows_of(i), i)
        send(remote(buf.at[p, 0], p, 1, rows_of(i), 3, i, 1))
        if i >= LAG:
            second_wave(i - LAG)
    for i in range(CHUNKS - LAG, CHUNKS):
        second_wave(i)
    for h in range(HALVES):
        half_tile(p, 0, h)
    for h in range(HALVES):
        for i in range(h * per, (h + 1) * per):
            landed(q, 1, rows_of(i), i)
        half_tile(q, 1, h)
    for i in range(CHUNKS - 1):
        pass_on(i)
        if i % per == per - 1:
            half_tile(q, 2, i // per)
    pass_on(CHUNKS - 1)
    half_tile(q, 2, HALVES - 1)
    for kind, slot in ((p, 1), (p, 2)):
        for h in range(HALVES):
            for i in range(h * per, (h + 1) * per):
                landed(kind, slot, rows_of(i), i)
            half_tile(kind, slot, h)

    loss_ref[...] = jnp.sum(losses[0].T, axis=0, keepdims=True) / (STEPS * count)
    for kind, out in ((0, gimg_ref), (1, gtxt_ref)):
        factor = inv[1 - kind][:, :1]
        unit = xin[1 - kind] * factor
        grad = acc[kind]
        along = jnp.sum(unit * grad, axis=-1, keepdims=True)
        out[...] = (grad - unit * along) * factor
    for copy, when in sent:
        if when is None:
            copy.wait_send()
        else:
            pl.when(when)(copy.wait_send)


def hand_over(*refs):
    half = (len(refs) - 1) // 2
    sem = refs[-1]
    copies = []
    for number, (src, dst) in enumerate(zip(refs[:half], refs[half:-1])):
        pieces = LOADS if src.shape[0] % LOADS == 0 else 1
        length = src.shape[0] // pieces
        for j in range(pieces):
            rows = pl.ds(j * length, length)
            copies.append(pltpu.make_async_copy(src.at[rows], dst.at[rows], sem.at[number, j]))
    for copy in copies:
        copy.start()
    for copy in copies:
        copy.wait()


def local(images, texts, log_temp, bias):
    count, width = images.shape
    block = jax.ShapeDtypeStruct((count, width), jnp.float32)
    vmem = pl.BlockSpec(memory_space=pltpu.VMEM)
    smem = pl.BlockSpec(memory_space=pltpu.SMEM)
    hbm = pl.BlockSpec(memory_space=pl.ANY)
    loss, gimg, gtxt = pl.pallas_call(
        kernel,
        out_shape=(jax.ShapeDtypeStruct((1, count), jnp.float32), block, block),
        in_specs=[hbm, hbm, smem, smem],
        out_specs=(vmem, vmem, vmem),
        scratch_shapes=[
            pltpu.VMEM((2, count, width), jnp.float32),
            pltpu.VMEM((2, count, width), jnp.bfloat16),
            pltpu.VMEM((2, STEPS - 1, count, width), jnp.bfloat16),
            pltpu.VMEM((2, count, width), jnp.float32),
            pltpu.VMEM((2, count, count // HALVES), jnp.float32),
            pltpu.VMEM((2, count, 128), jnp.float32),
            pltpu.SemaphoreType.DMA((2, LOADS)),
            pltpu.SemaphoreType.DMA((7, CHUNKS)),
            pltpu.SemaphoreType.DMA((2, STEPS - 1, CHUNKS)),
        ],
        compiler_params=pltpu.CompilerParams(
            collective_id=0, has_side_effects=True, vmem_limit_bytes=62 * 1024 * 1024),
    )(images, texts, log_temp, bias)
    results = (loss, gimg, gtxt)
    loss, gimg, gtxt = pl.pallas_call(
        hand_over,
        out_shape=tuple(jax.ShapeDtypeStruct(value.shape, value.dtype) for value in results),
        in_specs=[hbm] * 3,
        out_specs=(hbm,) * 3,
        scratch_shapes=[pltpu.SemaphoreType.DMA((3, LOADS))],
        compiler_params=pltpu.CompilerParams(vmem_limit_bytes=62 * 1024 * 1024),
    )(*results)
    return (loss.reshape(count), gimg, gtxt)


def solution(mesh):
    placed = (P(("dp", "rows"), None), P(("dp", "rows"), None), P(), P())
    return jax.shard_map(
        local,
        mesh=mesh,
        in_specs=placed,
        out_specs=(P(("dp", "rows")), P(("dp", "rows"), None), P(("dp", "rows"), None)),
        check_vma=False,
    )
```

```python
import functools

import jax
import jax.numpy as jnp
from jax import lax
from jax.experimental import pallas as pl
from jax.experimental.pallas import tpu as pltpu
from jax.sharding import PartitionSpec as P

STEPS = 4
CHUNKS = 8
HALVES = 2
LOADS = 4
PIECES = 4
LAG = 6
PEERS = (1, 2, 3, -1, -2, -3)
MESH = pl.DeviceIdType.MESH


def kernel(img_hbm, txt_hbm, temp_ref, bias_ref, loss_ref, grad_hbm,
           out_sem, xin, own, buf, acc, losses, inv, in_sem, send_sem, recv_sem):
    rows_n = lax.axis_size("rows")
    total = lax.axis_size("dp") * rows_n
    me = lax.axis_index("dp") * rows_n + lax.axis_index("rows")
    p = lax.rem(me, 2)
    q = 1 - p
    d = 1 - 2 * p
    count = own.shape[1]
    part = count // CHUNKS

    def peer(offset):
        place = lax.rem(me + offset * d + total, total)
        return (lax.div(place, rows_n), lax.rem(place, rows_n))

    barrier = pltpu.get_barrier_semaphore()
    for offset in PEERS:
        pl.semaphore_signal(barrier, inc=1, device_id=peer(offset), device_id_type=MESH)

    piece = count // LOADS

    def loading(source, kind, j):
        rows = pl.ds(j * piece, piece)
        return pltpu.make_async_copy(source.at[rows], xin.at[kind, rows], in_sem.at[kind, j])

    for j in range(LOADS):
        loading(txt_hbm, 0, j).start()
        loading(img_hbm, 1, j).start()

    def normalise(kind, j):
        rows = pl.ds(j * piece, piece)
        loading(txt_hbm, kind, j).wait()
        values = xin[kind, rows]
        scale_back = 1.0 / jnp.sqrt(jnp.sum(values * values, axis=-1, keepdims=True) + 1e-06)
        inv[kind, rows] = jnp.broadcast_to(scale_back, (piece, inv.shape[2]))
        own[kind, rows] = (values * scale_back).astype(jnp.bfloat16)

    line = rows_n // 2
    spot = lax.rem(lax.div(me, 2), line)

    def crosses(at, way):
        return jnp.logical_or(at + way < 0, at + way >= line)

    leaving = crosses(spot, d)
    direct = crosses(lax.rem(spot - d + line, line), -d)

    def rows_of(i):
        return pl.ds(i * part, part)

    def remote(src, kind, slot, rows, number, i, offset):
        return pltpu.make_async_remote_copy(
            src_ref=src.at[rows], dst_ref=buf.at[kind, slot, rows],
            send_sem=send_sem.at[number, i], recv_sem=recv_sem.at[kind, slot, i],
            device_id=peer(offset), device_id_type=MESH)

    def landed(kind, slot, rows, i):
        pltpu.make_async_remote_copy(
            src_ref=buf.at[kind, slot, rows], dst_ref=buf.at[kind, slot, rows],
            send_sem=send_sem.at[0, i], recv_sem=recv_sem.at[kind, slot, i],
            device_id=peer(1), device_id_type=MESH).wait_recv()

    everything = pl.ds(0, count)
    scale = jnp.exp(jnp.full((1, 1), temp_ref[0], jnp.float32))
    shift = bias_ref[0]

    def tile(kind, visit, first):
        other = visit[...]
        dots = lax.dot_general(own[1 - kind], other, (((1,), (1,)), ((), ())),
                               preferred_element_type=jnp.float32)
        z = scale * dots + shift
        if first:
            eye = (lax.broadcasted_iota(jnp.int32, z.shape, 0)
                   == lax.broadcasted_iota(jnp.int32, z.shape, 1))
            z = jnp.where(eye, -z, z)
        e = jnp.exp(z)
        more = 1.0 + e
        soft = jnp.log(more)
        slope = (e / more) * scale
        if first:
            slope = jnp.where(eye, -slope, slope)
        wide = losses.shape[2]
        folded = soft[:, :wide]
        if first:
            for at in range(wide, count, wide):
                folded = folded + soft[:, at:at + wide]
        grad = jnp.dot(slope.astype(jnp.bfloat16), other, preferred_element_type=jnp.float32)
        if first:
            losses[kind] = folded
            acc[kind] = grad
        else:
            losses[kind] = losses[kind] + folded
            acc[kind] = acc[kind] + grad

    def result(kind, j):
        rows = pl.ds(j * piece, piece)
        return pltpu.make_async_copy(acc.at[kind, rows], grad_hbm.at[kind, rows], out_sem.at[kind, j])

    def finish(kind):
        for j in range(LOADS):
            rows = pl.ds(j * piece, piece)
            factor = inv[1 - kind, rows][:, :1]
            unit = xin[1 - kind, rows] * factor
            grad = acc[kind, rows]
            along = jnp.sum(unit * grad, axis=-1, keepdims=True)
            acc[kind, rows] = (grad - unit * along) * factor
            result(kind, j).start()

    sent = []

    def send(copy, when=None):
        if when is None:
            copy.start()
        else:
            pl.when(when)(copy.start)
        sent.append((copy, when))

    for j in range(LOADS):
        normalise(q, j)
    pl.semaphore_wait(barrier, len(PEERS))
    for i in range(CHUNKS):
        send(remote(own.at[q], q, 0, rows_of(i), 0, i, -1))
    for j in range(LOADS):
        normalise(p, j)
    send(remote(own.at[p], p, 0, everything, 1, 0, 1))

    tile(0, own.at[0], True)
    tile(1, own.at[1], True)
    span = count // HALVES

    def half_tile(kind, slot, h):
        tile(kind, buf.at[kind, slot, pl.ds(h * span, span)], False)

    landed(q, 0, everything, 0)
    for h in range(HALVES):
        half_tile(q, 0, h)

    staying = jnp.logical_not(leaving)
    per = CHUNKS // HALVES

    def second_wave(i):
        rows = rows_of(i)
        send(remote(buf.at[p, 0], p, 2, rows, 2, i, 2), staying)
        send(remote(own.at[p], p, 2, rows, 4, i, 3))
        send(remote(own.at[q], q, 2, rows, 6, i, -3), direct)

    def pass_on(i):
        landed(q, 2, rows_of(i), i)
        send(remote(buf.at[q, 2], q, 1, rows_of(i), 5, i, 1))

    for i in range(CHUNKS):
        landed(p, 0, rows_of(i), i)
        send(remote(buf.at[p, 0], p, 1, rows_of(i), 3, i, 1))
        if i >= LAG:
            second_wave(i - LAG)
    for i in range(CHUNKS - LAG, CHUNKS):
        second_wave(i)
    for h in range(HALVES):
        half_tile(p, 0, h)
    for h in range(HALVES):
        for i in range(h * per, (h + 1) * per):
            landed(q, 1, rows_of(i), i)
        half_tile(q, 1, h)
    for i in range(CHUNKS - 1):
        pass_on(i)
        if i % per == per - 1:
            half_tile(q, 2, i // per)
    pass_on(CHUNKS - 1)
    half_tile(q, 2, HALVES - 1)
    finish(q)
    for kind, slot in ((p, 1), (p, 2)):
        for h in range(HALVES):
            for i in range(h * per, (h + 1) * per):
                landed(kind, slot, rows_of(i), i)
            half_tile(kind, slot, h)

    loss_ref[...] = jnp.sum(losses[0].T, axis=0, keepdims=True) / (STEPS * count)
    finish(p)
    for copy, when in sent:
        if when is None:
            copy.wait_send()
        else:
            pl.when(when)(copy.wait_send)
    for kind in (q, p):
        for j in range(LOADS):
            result(kind, j).wait()


def hand_over(loss_ref, grad_hbm, row_ref, gimg_hbm, gtxt_hbm, held, in_sem, out_sem):
    piece = held.shape[1] // PIECES
    outs = (gimg_hbm, gtxt_hbm)
    order = [(kind, j) for kind in range(2) for j in range(PIECES)]

    def into(kind, j):
        rows = pl.ds(j * piece, piece)
        return pltpu.make_async_copy(grad_hbm.at[kind, rows], held.at[kind, rows], in_sem.at[kind, j])

    def out_of(kind, j):
        rows = pl.ds(j * piece, piece)
        return pltpu.make_async_copy(held.at[kind, rows], outs[kind].at[rows], out_sem.at[kind, j])

    for at in order:
        into(*at).start()
    row_ref[...] = loss_ref[...]
    for at in order:
        into(*at).wait()
        out_of(*at).start()
    for at in order:
        out_of(*at).wait()


def local(images, texts, log_temp, bias):
    count, width = images.shape
    block = jax.ShapeDtypeStruct((count, width), jnp.float32)
    vmem = pl.BlockSpec(memory_space=pltpu.VMEM)
    smem = pl.BlockSpec(memory_space=pltpu.SMEM)
    hbm = pl.BlockSpec(memory_space=pl.ANY)
    loss, grads = pl.pallas_call(
        kernel,
        out_shape=(jax.ShapeDtypeStruct((1, count), jnp.float32),
                   jax.ShapeDtypeStruct((2, count, width), jnp.float32)),
        in_specs=[hbm, hbm, smem, smem],
        out_specs=(vmem, hbm),
        scratch_shapes=[
            pltpu.SemaphoreType.DMA((2, LOADS)),
            pltpu.VMEM((2, count, width), jnp.float32),
            pltpu.VMEM((2, count, width), jnp.bfloat16),
            pltpu.VMEM((2, STEPS - 1, count, width), jnp.bfloat16),
            pltpu.VMEM((2, count, width), jnp.float32),
            pltpu.VMEM((2, count, count // HALVES), jnp.float32),
            pltpu.VMEM((2, count, 128), jnp.float32),
            pltpu.SemaphoreType.DMA((2, LOADS)),
            pltpu.SemaphoreType.DMA((7, CHUNKS)),
            pltpu.SemaphoreType.DMA((2, STEPS - 1, CHUNKS)),
        ],
        compiler_params=pltpu.CompilerParams(
            collective_id=0, has_side_effects=True, vmem_limit_bytes=62 * 1024 * 1024),
    )(images, texts, log_temp, bias)
    loss, gimg, gtxt = pl.pallas_call(
        hand_over,
        out_shape=(jax.ShapeDtypeStruct((1, count), jnp.float32), block, block),
        in_specs=[vmem, hbm],
        out_specs=(vmem, hbm, hbm),
        scratch_shapes=[
            pltpu.VMEM((2, count, width), jnp.float32),
            pltpu.SemaphoreType.DMA((2, PIECES)),
            pltpu.SemaphoreType.DMA((2, PIECES)),
        ],
        compiler_params=pltpu.CompilerParams(vmem_limit_bytes=62 * 1024 * 1024),
    )(loss, grads)
    return (loss.reshape(count), gimg, gtxt)


def solution(mesh):
    placed = (P(("dp", "rows"), None), P(("dp", "rows"), None), P(), P())
    return jax.shard_map(
        local,
        mesh=mesh,
        in_specs=placed,
        out_specs=(P(("dp", "rows")), P(("dp", "rows"), None), P(("dp", "rows"), None)),
        check_vma=False,
    )
```

```python
import functools

import jax
import jax.numpy as jnp
from jax import lax
from jax.experimental import pallas as pl
from jax.experimental.pallas import tpu as pltpu
from jax.sharding import PartitionSpec as P

STEPS = 4
CHUNKS = 8
HALVES = 2
PIECES = 4
LAG = 6
PEERS = (1, 2, 3, -1, -2, -3)
MESH = pl.DeviceIdType.MESH


def kernel(img_ref, txt_ref, temp_ref, bias_ref, loss_ref, acc,
           own, buf, losses, inv, send_sem, recv_sem):
    rows_n = lax.axis_size("rows")
    total = lax.axis_size("dp") * rows_n
    me = lax.axis_index("dp") * rows_n + lax.axis_index("rows")
    p = lax.rem(me, 2)
    q = 1 - p
    d = 1 - 2 * p
    count = own.shape[1]
    part = count // CHUNKS

    def peer(offset):
        place = lax.rem(me + offset * d + total, total)
        return (lax.div(place, rows_n), lax.rem(place, rows_n))

    barrier = pltpu.get_barrier_semaphore()
    for offset in PEERS:
        pl.semaphore_signal(barrier, inc=1, device_id=peer(offset), device_id_type=MESH)

    given = (txt_ref, img_ref)

    def normalise(kind):
        values = given[kind][...]
        scale_back = 1.0 / jnp.sqrt(jnp.sum(values * values, axis=-1, keepdims=True) + 1e-06)
        inv[kind] = jnp.broadcast_to(scale_back, inv.shape[1:])
        own[kind] = (values * scale_back).astype(jnp.bfloat16)

    line = rows_n // 2
    spot = lax.rem(lax.div(me, 2), line)

    def crosses(at, way):
        return jnp.logical_or(at + way < 0, at + way >= line)

    leaving = crosses(spot, d)
    direct = crosses(lax.rem(spot - d + line, line), -d)

    def rows_of(i):
        return pl.ds(i * part, part)

    def remote(src, kind, slot, rows, number, i, offset):
        return pltpu.make_async_remote_copy(
            src_ref=src.at[rows], dst_ref=buf.at[kind, slot, rows],
            send_sem=send_sem.at[number, i], recv_sem=recv_sem.at[kind, slot, i],
            device_id=peer(offset), device_id_type=MESH)

    def landed(kind, slot, rows, i):
        pltpu.make_async_remote_copy(
            src_ref=buf.at[kind, slot, rows], dst_ref=buf.at[kind, slot, rows],
            send_sem=send_sem.at[0, i], recv_sem=recv_sem.at[kind, slot, i],
            device_id=peer(1), device_id_type=MESH).wait_recv()

    everything = pl.ds(0, count)
    scale = jnp.exp(jnp.full((1, 1), temp_ref[0], jnp.float32))
    shift = bias_ref[0]

    def tile(kind, visit, first):
        other = visit[...]
        dots = lax.dot_general(own[1 - kind], other, (((1,), (1,)), ((), ())),
                               preferred_element_type=jnp.float32)
        z = scale * dots + shift
        if first:
            eye = (lax.broadcasted_iota(jnp.int32, z.shape, 0)
                   == lax.broadcasted_iota(jnp.int32, z.shape, 1))
            z = jnp.where(eye, -z, z)
        e = jnp.exp(z)
        more = 1.0 + e
        soft = jnp.log(more)
        slope = (e / more) * scale
        if first:
            slope = jnp.where(eye, -slope, slope)
        wide = losses.shape[2]
        folded = soft[:, :wide]
        if first:
            for at in range(wide, count, wide):
                folded = folded + soft[:, at:at + wide]
        grad = jnp.dot(slope.astype(jnp.bfloat16), other, preferred_element_type=jnp.float32)
        if first:
            losses[kind] = folded
            acc[kind] = grad
        else:
            losses[kind] = losses[kind] + folded
            acc[kind] = acc[kind] + grad

    def finish(kind):
        factor = inv[1 - kind][:, :1]
        unit = given[1 - kind][...] * factor
        grad = acc[kind]
        along = jnp.sum(unit * grad, axis=-1, keepdims=True)
        acc[kind] = (grad - unit * along) * factor

    def finish_one(dynamic):
        for kind in range(2):
            pl.when(dynamic == kind)(functools.partial(finish, kind))

    sent = []

    def send(copy, when=None):
        if when is None:
            copy.start()
        else:
            pl.when(when)(copy.start)
        sent.append((copy, when))

    normalise(0)
    normalise(1)
    pl.semaphore_wait(barrier, len(PEERS))
    for i in range(CHUNKS):
        send(remote(own.at[q], q, 0, rows_of(i), 0, i, -1))
    send(remote(own.at[p], p, 0, everything, 1, 0, 1))

    tile(0, own.at[0], True)
    tile(1, own.at[1], True)
    span = count // HALVES

    def half_tile(kind, slot, h):
        tile(kind, buf.at[kind, slot, pl.ds(h * span, span)], False)

    landed(q, 0, everything, 0)
    for h in range(HALVES):
        half_tile(q, 0, h)

    staying = jnp.logical_not(leaving)
    per = CHUNKS // HALVES

    def second_wave(i):
        rows = rows_of(i)
        send(remote(buf.at[p, 0], p, 2, rows, 2, i, 2), staying)
        send(remote(own.at[p], p, 2, rows, 4, i, 3))
        send(remote(own.at[q], q, 2, rows, 6, i, -3), direct)

    def pass_on(i):
        landed(q, 2, rows_of(i), i)
        send(remote(buf.at[q, 2], q, 1, rows_of(i), 5, i, 1))

    for i in range(CHUNKS):
        landed(p, 0, rows_of(i), i)
        send(remote(buf.at[p, 0], p, 1, rows_of(i), 3, i, 1))
        if i >= LAG:
            second_wave(i - LAG)
    for i in range(CHUNKS - LAG, CHUNKS):
        second_wave(i)
    for h in range(HALVES):
        half_tile(p, 0, h)
    for h in range(HALVES):
        for i in range(h * per, (h + 1) * per):
            landed(q, 1, rows_of(i), i)
        half_tile(q, 1, h)
    for i in range(CHUNKS - 1):
        pass_on(i)
        if i % per == per - 1:
            half_tile(q, 2, i // per)
    pass_on(CHUNKS - 1)
    half_tile(q, 2, HALVES - 1)
    finish_one(q)
    for kind, slot in ((p, 1), (p, 2)):
        for h in range(HALVES):
            for i in range(h * per, (h + 1) * per):
                landed(kind, slot, rows_of(i), i)
            half_tile(kind, slot, h)

    loss_ref[...] = jnp.sum(losses[0].T, axis=0, keepdims=True) / (STEPS * count)
    finish_one(p)
    for copy, when in sent:
        if when is None:
            copy.wait_send()
        else:
            pl.when(when)(copy.wait_send)


def hand_over(loss_ref, grad_ref, row_ref, gimg_hbm, gtxt_hbm, sem):
    piece = grad_ref.shape[1] // PIECES
    copies = []
    for kind, out in enumerate((gimg_hbm, gtxt_hbm)):
        for j in range(PIECES):
            rows = pl.ds(j * piece, piece)
            copies.append(pltpu.make_async_copy(grad_ref.at[kind, rows], out.at[rows], sem.at[kind, j]))
    for copy in copies:
        copy.start()
    row_ref[...] = loss_ref[...]
    for copy in copies:
        copy.wait()


def local(images, texts, log_temp, bias):
    count, width = images.shape
    block = jax.ShapeDtypeStruct((count, width), jnp.float32)
    vmem = pl.BlockSpec(memory_space=pltpu.VMEM)
    smem = pl.BlockSpec(memory_space=pltpu.SMEM)
    hbm = pl.BlockSpec(memory_space=pl.ANY)
    loss, grads = pl.pallas_call(
        kernel,
        out_shape=(jax.ShapeDtypeStruct((1, count), jnp.float32),
                   jax.ShapeDtypeStruct((2, count, width), jnp.float32)),
        in_specs=[vmem, vmem, smem, smem],
        out_specs=(vmem, vmem),
        scratch_shapes=[
            pltpu.VMEM((2, count, width), jnp.bfloat16),
            pltpu.VMEM((2, STEPS - 1, count, width), jnp.bfloat16),
            pltpu.VMEM((2, count, count // HALVES), jnp.float32),
            pltpu.VMEM((2, count, 128), jnp.float32),
            pltpu.SemaphoreType.DMA((7, CHUNKS)),
            pltpu.SemaphoreType.DMA((2, STEPS - 1, CHUNKS)),
        ],
        compiler_params=pltpu.CompilerParams(
            collective_id=0, has_side_effects=True, vmem_limit_bytes=48 * 1024 * 1024),
    )(images, texts, log_temp, bias)
    loss, gimg, gtxt = pl.pallas_call(
        hand_over,
        out_shape=(jax.ShapeDtypeStruct((1, count), jnp.float32), block, block),
        in_specs=[vmem, vmem],
        out_specs=(vmem, hbm, hbm),
        scratch_shapes=[
            pltpu.SemaphoreType.DMA((2, PIECES)),
        ],
        compiler_params=pltpu.CompilerParams(vmem_limit_bytes=16 * 1024 * 1024),
    )(loss, grads)
    return (loss.reshape(count), gimg, gtxt)


def solution(mesh):
    placed = (P(("dp", "rows"), None), P(("dp", "rows"), None), P(), P())
    return jax.shard_map(
        local,
        mesh=mesh,
        in_specs=placed,
        out_specs=(P(("dp", "rows")), P(("dp", "rows"), None), P(("dp", "rows"), None)),
        check_vma=False,
    )
```

```python
import functools

import jax
import jax.numpy as jnp
from jax import lax
from jax.experimental import pallas as pl
from jax.experimental.pallas import tpu as pltpu
from jax.sharding import PartitionSpec as P

STEPS = 4
CHUNKS = 8
HALVES = 2
PIECES = 4
FAR_LAG = 3
NEAR_LAG = 6
PEERS = (1, 2, 3, -1, -2, -3)
MESH = pl.DeviceIdType.MESH


def kernel(img_ref, txt_ref, temp_ref, bias_ref, loss_ref, acc,
           own, buf, losses, inv, send_sem, recv_sem):
    rows_n = lax.axis_size("rows")
    total = lax.axis_size("dp") * rows_n
    me = lax.axis_index("dp") * rows_n + lax.axis_index("rows")
    p = lax.rem(me, 2)
    q = 1 - p
    d = 1 - 2 * p
    count = own.shape[1]
    part = count // CHUNKS

    def peer(offset):
        place = lax.rem(me + offset * d + total, total)
        return (lax.div(place, rows_n), lax.rem(place, rows_n))

    barrier = pltpu.get_barrier_semaphore()
    for offset in PEERS:
        pl.semaphore_signal(barrier, inc=1, device_id=peer(offset), device_id_type=MESH)

    given = (txt_ref, img_ref)

    def normalise(kind):
        values = given[kind][...]
        scale_back = 1.0 / jnp.sqrt(jnp.sum(values * values, axis=-1, keepdims=True) + 1e-06)
        inv[kind] = jnp.broadcast_to(scale_back, inv.shape[1:])
        own[kind] = (values * scale_back).astype(jnp.bfloat16)

    line = rows_n // 2
    spot = lax.rem(lax.div(me, 2), line)

    def crosses(at, way):
        return jnp.logical_or(at + way < 0, at + way >= line)

    leaving = crosses(spot, d)
    direct = crosses(lax.rem(spot - d + line, line), -d)

    def rows_of(i):
        return pl.ds(i * part, part)

    def remote(src, kind, slot, rows, number, i, offset):
        return pltpu.make_async_remote_copy(
            src_ref=src.at[rows], dst_ref=buf.at[kind, slot, rows],
            send_sem=send_sem.at[number, i], recv_sem=recv_sem.at[kind, slot, i],
            device_id=peer(offset), device_id_type=MESH)

    def landed(kind, slot, rows, i):
        pltpu.make_async_remote_copy(
            src_ref=buf.at[kind, slot, rows], dst_ref=buf.at[kind, slot, rows],
            send_sem=send_sem.at[0, i], recv_sem=recv_sem.at[kind, slot, i],
            device_id=peer(1), device_id_type=MESH).wait_recv()

    everything = pl.ds(0, count)
    scale = jnp.exp(jnp.full((1, 1), temp_ref[0], jnp.float32))
    shift = bias_ref[0]

    def tile(kind, visit, first):
        other = visit[...]
        dots = lax.dot_general(own[1 - kind], other, (((1,), (1,)), ((), ())),
                               preferred_element_type=jnp.float32)
        z = scale * dots + shift
        if first:
            eye = (lax.broadcasted_iota(jnp.int32, z.shape, 0)
                   == lax.broadcasted_iota(jnp.int32, z.shape, 1))
            z = jnp.where(eye, -z, z)
        e = jnp.exp(z)
        more = 1.0 + e
        soft = jnp.log(more)
        slope = (e / more) * scale
        if first:
            slope = jnp.where(eye, -slope, slope)
        wide = losses.shape[2]
        folded = soft[:, :wide]
        if first:
            for at in range(wide, count, wide):
                folded = folded + soft[:, at:at + wide]
        grad = jnp.dot(slope.astype(jnp.bfloat16), other, preferred_element_type=jnp.float32)
        if first:
            losses[kind] = folded
            acc[kind] = grad
        else:
            losses[kind] = losses[kind] + folded
            acc[kind] = acc[kind] + grad

    def finish(kind):
        factor = inv[1 - kind][:, :1]
        unit = given[1 - kind][...] * factor
        grad = acc[kind]
        along = jnp.sum(unit * grad, axis=-1, keepdims=True)
        acc[kind] = (grad - unit * along) * factor

    def finish_one(dynamic):
        for kind in range(2):
            pl.when(dynamic == kind)(functools.partial(finish, kind))

    sent = []

    def send(copy, when=None):
        if when is None:
            copy.start()
        else:
            pl.when(when)(copy.start)
        sent.append((copy, when))

    normalise(0)
    normalise(1)
    pl.semaphore_wait(barrier, len(PEERS))
    for i in range(CHUNKS):
        send(remote(own.at[q], q, 0, rows_of(i), 0, i, -1))
    send(remote(own.at[p], p, 0, everything, 1, 0, 1))

    tile(0, own.at[0], True)
    tile(1, own.at[1], True)
    span = count // HALVES

    def half_tile(kind, slot, h):
        tile(kind, buf.at[kind, slot, pl.ds(h * span, span)], False)

    landed(q, 0, everything, 0)
    for h in range(HALVES):
        half_tile(q, 0, h)

    staying = jnp.logical_not(leaving)
    per = CHUNKS // HALVES

    def far_wave(i):
        rows = rows_of(i)
        send(remote(own.at[q], q, 2, rows, 6, i, -3), direct)
        pl.when(leaving)(remote(own.at[p], p, 2, rows, 4, i, 3).start)

    def near_wave(i):
        rows = rows_of(i)
        send(remote(buf.at[p, 0], p, 2, rows, 2, i, 2), staying)
        own_copy = remote(own.at[p], p, 2, rows, 4, i, 3)
        pl.when(staying)(own_copy.start)
        sent.append((own_copy, None))

    def pass_on(i):
        landed(q, 2, rows_of(i), i)
        send(remote(buf.at[q, 2], q, 1, rows_of(i), 5, i, 1))

    for i in range(CHUNKS):
        landed(p, 0, rows_of(i), i)
        send(remote(buf.at[p, 0], p, 1, rows_of(i), 3, i, 1))
        if i >= FAR_LAG:
            far_wave(i - FAR_LAG)
        if i >= NEAR_LAG:
            near_wave(i - NEAR_LAG)
    for i in range(CHUNKS - FAR_LAG, CHUNKS):
        far_wave(i)
    for i in range(CHUNKS - NEAR_LAG, CHUNKS):
        near_wave(i)
    for h in range(HALVES):
        half_tile(p, 0, h)
    for h in range(HALVES):
        for i in range(h * per, (h + 1) * per):
            landed(q, 1, rows_of(i), i)
        half_tile(q, 1, h)
    for i in range(CHUNKS - 1):
        pass_on(i)
        if i % per == per - 1:
            half_tile(q, 2, i // per)
    pass_on(CHUNKS - 1)
    half_tile(q, 2, HALVES - 1)
    finish_one(q)
    for kind, slot in ((p, 1), (p, 2)):
        for h in range(HALVES):
            for i in range(h * per, (h + 1) * per):
                landed(kind, slot, rows_of(i), i)
            half_tile(kind, slot, h)

    loss_ref[...] = jnp.sum(losses[0].T, axis=0, keepdims=True) / (STEPS * count)
    finish_one(p)
    for copy, when in sent:
        if when is None:
            copy.wait_send()
        else:
            pl.when(when)(copy.wait_send)


def hand_over(loss_ref, grad_ref, row_ref, gimg_hbm, gtxt_hbm, sem):
    piece = grad_ref.shape[1] // PIECES
    copies = []
    for kind, out in enumerate((gimg_hbm, gtxt_hbm)):
        for j in range(PIECES):
            rows = pl.ds(j * piece, piece)
            copies.append(pltpu.make_async_copy(grad_ref.at[kind, rows], out.at[rows], sem.at[kind, j]))
    for copy in copies:
        copy.start()
    row_ref[...] = loss_ref[...]
    for copy in copies:
        copy.wait()


def local(images, texts, log_temp, bias):
    count, width = images.shape
    block = jax.ShapeDtypeStruct((count, width), jnp.float32)
    vmem = pl.BlockSpec(memory_space=pltpu.VMEM)
    smem = pl.BlockSpec(memory_space=pltpu.SMEM)
    hbm = pl.BlockSpec(memory_space=pl.ANY)
    loss, grads = pl.pallas_call(
        kernel,
        out_shape=(jax.ShapeDtypeStruct((1, count), jnp.float32),
                   jax.ShapeDtypeStruct((2, count, width), jnp.float32)),
        in_specs=[vmem, vmem, smem, smem],
        out_specs=(vmem, vmem),
        scratch_shapes=[
            pltpu.VMEM((2, count, width), jnp.bfloat16),
            pltpu.VMEM((2, STEPS - 1, count, width), jnp.bfloat16),
            pltpu.VMEM((2, count, count // HALVES), jnp.float32),
            pltpu.VMEM((2, count, 128), jnp.float32),
            pltpu.SemaphoreType.DMA((7, CHUNKS)),
            pltpu.SemaphoreType.DMA((2, STEPS - 1, CHUNKS)),
        ],
        compiler_params=pltpu.CompilerParams(
            collective_id=0, has_side_effects=True, vmem_limit_bytes=48 * 1024 * 1024),
    )(images, texts, log_temp, bias)
    loss, gimg, gtxt = pl.pallas_call(
        hand_over,
        out_shape=(jax.ShapeDtypeStruct((1, count), jnp.float32), block, block),
        in_specs=[vmem, vmem],
        out_specs=(vmem, hbm, hbm),
        scratch_shapes=[
            pltpu.SemaphoreType.DMA((2, PIECES)),
        ],
        compiler_params=pltpu.CompilerParams(vmem_limit_bytes=16 * 1024 * 1024),
    )(loss, grads)
    return (loss.reshape(count), gimg, gtxt)


def solution(mesh):
    placed = (P(("dp", "rows"), None), P(("dp", "rows"), None), P(), P())
    return jax.shard_map(
        local,
        mesh=mesh,
        in_specs=placed,
        out_specs=(P(("dp", "rows")), P(("dp", "rows"), None), P(("dp", "rows"), None)),
        check_vma=False,
    )
```

```python
import functools

import jax
import jax.numpy as jnp
from jax import lax
from jax.experimental import pallas as pl
from jax.experimental.pallas import tpu as pltpu
from jax.sharding import PartitionSpec as P

STEPS = 4
CHUNKS = 8
HALVES = 2
PIECES = 4
FAR_LAG = 3
NEAR_LAG = 6
PEERS = (1, 2, 3, -1, -2, -3)
MESH = pl.DeviceIdType.MESH


def kernel(img_ref, txt_ref, temp_ref, bias_ref, loss_ref, acc,
           own, buf, losses, inv, send_sem, recv_sem):
    rows_n = lax.axis_size("rows")
    total = lax.axis_size("dp") * rows_n
    me = lax.axis_index("dp") * rows_n + lax.axis_index("rows")
    p = lax.rem(me, 2)
    q = 1 - p
    d = 1 - 2 * p
    count = own.shape[1]
    part = count // CHUNKS

    def peer(offset):
        place = lax.rem(me + offset * d + total, total)
        return (lax.div(place, rows_n), lax.rem(place, rows_n))

    barrier = pltpu.get_barrier_semaphore()
    for offset in PEERS:
        pl.semaphore_signal(barrier, inc=1, device_id=peer(offset), device_id_type=MESH)

    given = (txt_ref, img_ref)

    def normalise(kind):
        values = given[kind][...]
        scale_back = 1.0 / jnp.sqrt(jnp.sum(values * values, axis=-1, keepdims=True) + 1e-06)
        inv[kind] = jnp.broadcast_to(scale_back, inv.shape[1:])
        own[kind] = (values * scale_back).astype(jnp.bfloat16)

    line = rows_n // 2
    spot = lax.rem(lax.div(me, 2), line)

    def crosses(at, way):
        return jnp.logical_or(at + way < 0, at + way >= line)

    leaving = crosses(spot, d)
    direct = crosses(lax.rem(spot - d + line, line), -d)

    def rows_of(i):
        return pl.ds(i * part, part)

    def remote(src, kind, slot, rows, number, i, offset):
        return pltpu.make_async_remote_copy(
            src_ref=src.at[rows], dst_ref=buf.at[kind, slot, rows],
            send_sem=send_sem.at[number, i], recv_sem=recv_sem.at[kind, slot, i],
            device_id=peer(offset), device_id_type=MESH)

    def landed(kind, slot, rows, i):
        pltpu.make_async_remote_copy(
            src_ref=buf.at[kind, slot, rows], dst_ref=buf.at[kind, slot, rows],
            send_sem=send_sem.at[0, i], recv_sem=recv_sem.at[kind, slot, i],
            device_id=peer(1), device_id_type=MESH).wait_recv()

    everything = pl.ds(0, count)
    scale = jnp.exp(jnp.full((1, 1), temp_ref[0], jnp.float32))
    shift = bias_ref[0]

    def tile(kind, visit, first):
        other = visit[...]
        dots = lax.dot_general(own[1 - kind], other, (((1,), (1,)), ((), ())),
                               preferred_element_type=jnp.float32)
        z = scale * dots + shift
        if first:
            eye = (lax.broadcasted_iota(jnp.int32, z.shape, 0)
                   == lax.broadcasted_iota(jnp.int32, z.shape, 1))
            z = jnp.where(eye, -z, z)
        e = jnp.exp(z)
        more = 1.0 + e
        soft = jnp.log(more)
        slope = (e / more) * scale
        if first:
            slope = jnp.where(eye, -slope, slope)
        wide = losses.shape[2]
        folded = soft[:, :wide]
        if first:
            for at in range(wide, count, wide):
                folded = folded + soft[:, at:at + wide]
        grad = jnp.dot(slope.astype(jnp.bfloat16), other, preferred_element_type=jnp.float32)
        if first:
            losses[kind] = folded
            acc[kind] = grad
        else:
            losses[kind] = losses[kind] + folded
            acc[kind] = acc[kind] + grad

    def finish(kind):
        factor = inv[1 - kind][:, :1]
        unit = given[1 - kind][...] * factor
        grad = acc[kind]
        along = jnp.sum(unit * grad, axis=-1, keepdims=True)
        acc[kind] = (grad - unit * along) * factor

    def finish_one(dynamic):
        for kind in range(2):
            pl.when(dynamic == kind)(functools.partial(finish, kind))

    sent = []

    def send(copy, when=None):
        if when is None:
            copy.start()
        else:
            pl.when(when)(copy.start)
        sent.append((copy, when))

    def normalise_one(dynamic):
        for kind in range(2):
            pl.when(dynamic == kind)(functools.partial(normalise, kind))

    normalise_one(q)
    pl.semaphore_wait(barrier, len(PEERS))
    for i in range(CHUNKS):
        send(remote(own.at[q], q, 0, rows_of(i), 0, i, -1))
    normalise_one(p)
    send(remote(own.at[p], p, 0, everything, 1, 0, 1))

    tile(0, own.at[0], True)
    tile(1, own.at[1], True)
    span = count // HALVES

    def half_tile(kind, slot, h):
        tile(kind, buf.at[kind, slot, pl.ds(h * span, span)], False)

    landed(q, 0, everything, 0)
    for h in range(HALVES):
        half_tile(q, 0, h)

    staying = jnp.logical_not(leaving)
    per = CHUNKS // HALVES

    def far_wave(i):
        rows = rows_of(i)
        send(remote(own.at[q], q, 2, rows, 6, i, -3), direct)
        pl.when(leaving)(remote(own.at[p], p, 2, rows, 4, i, 3).start)

    def near_wave(i):
        rows = rows_of(i)
        send(remote(buf.at[p, 0], p, 2, rows, 2, i, 2), staying)
        own_copy = remote(own.at[p], p, 2, rows, 4, i, 3)
        pl.when(staying)(own_copy.start)
        sent.append((own_copy, None))

    def pass_on(i):
        landed(q, 2, rows_of(i), i)
        send(remote(buf.at[q, 2], q, 1, rows_of(i), 5, i, 1))

    for i in range(CHUNKS):
        landed(p, 0, rows_of(i), i)
        send(remote(buf.at[p, 0], p, 1, rows_of(i), 3, i, 1))
        if i >= FAR_LAG:
            far_wave(i - FAR_LAG)
        if i >= NEAR_LAG:
            near_wave(i - NEAR_LAG)
    for i in range(CHUNKS - FAR_LAG, CHUNKS):
        far_wave(i)
    for i in range(CHUNKS - NEAR_LAG, CHUNKS):
        near_wave(i)
    for h in range(HALVES):
        half_tile(p, 0, h)
    for h in range(HALVES):
        for i in range(h * per, (h + 1) * per):
            landed(q, 1, rows_of(i), i)
        half_tile(q, 1, h)
    for i in range(CHUNKS - 1):
        pass_on(i)
        if i % per == per - 1:
            half_tile(q, 2, i // per)
    pass_on(CHUNKS - 1)
    half_tile(q, 2, HALVES - 1)
    finish_one(q)
    for kind, slot in ((p, 1), (p, 2)):
        for h in range(HALVES):
            for i in range(h * per, (h + 1) * per):
                landed(kind, slot, rows_of(i), i)
            half_tile(kind, slot, h)

    loss_ref[...] = jnp.sum(losses[0].T, axis=0, keepdims=True) / (STEPS * count)
    finish_one(p)
    for copy, when in sent:
        if when is None:
            copy.wait_send()
        else:
            pl.when(when)(copy.wait_send)


def hand_over(loss_ref, grad_ref, row_ref, gimg_hbm, gtxt_hbm, sem):
    piece = grad_ref.shape[1] // PIECES
    copies = []
    for kind, out in enumerate((gimg_hbm, gtxt_hbm)):
        for j in range(PIECES):
            rows = pl.ds(j * piece, piece)
            copies.append(pltpu.make_async_copy(grad_ref.at[kind, rows], out.at[rows], sem.at[kind, j]))
    for copy in copies:
        copy.start()
    row_ref[...] = loss_ref[...]
    for copy in copies:
        copy.wait()


def local(images, texts, log_temp, bias):
    count, width = images.shape
    block = jax.ShapeDtypeStruct((count, width), jnp.float32)
    vmem = pl.BlockSpec(memory_space=pltpu.VMEM)
    smem = pl.BlockSpec(memory_space=pltpu.SMEM)
    hbm = pl.BlockSpec(memory_space=pl.ANY)
    loss, grads = pl.pallas_call(
        kernel,
        out_shape=(jax.ShapeDtypeStruct((1, count), jnp.float32),
                   jax.ShapeDtypeStruct((2, count, width), jnp.float32)),
        in_specs=[vmem, vmem, smem, smem],
        out_specs=(vmem, vmem),
        scratch_shapes=[
            pltpu.VMEM((2, count, width), jnp.bfloat16),
            pltpu.VMEM((2, STEPS - 1, count, width), jnp.bfloat16),
            pltpu.VMEM((2, count, count // HALVES), jnp.float32),
            pltpu.VMEM((2, count, 128), jnp.float32),
            pltpu.SemaphoreType.DMA((7, CHUNKS)),
            pltpu.SemaphoreType.DMA((2, STEPS - 1, CHUNKS)),
        ],
        compiler_params=pltpu.CompilerParams(
            collective_id=0, has_side_effects=True, vmem_limit_bytes=48 * 1024 * 1024),
    )(images, texts, log_temp, bias)
    loss, gimg, gtxt = pl.pallas_call(
        hand_over,
        out_shape=(jax.ShapeDtypeStruct((1, count), jnp.float32), block, block),
        in_specs=[vmem, vmem],
        out_specs=(vmem, hbm, hbm),
        scratch_shapes=[
            pltpu.SemaphoreType.DMA((2, PIECES)),
        ],
        compiler_params=pltpu.CompilerParams(vmem_limit_bytes=16 * 1024 * 1024),
    )(loss, grads)
    return (loss.reshape(count), gimg, gtxt)


def solution(mesh):
    placed = (P(("dp", "rows"), None), P(("dp", "rows"), None), P(), P())
    return jax.shard_map(
        local,
        mesh=mesh,
        in_specs=placed,
        out_specs=(P(("dp", "rows")), P(("dp", "rows"), None), P(("dp", "rows"), None)),
        check_vma=False,
    )
```
